32 devices in a mesh: parts: 2 (over y), blk: 4 (over z), dp: 2 (over x), sub: 2 (over core).
Axes of the slice: x: 2, y: 2, z: 4, core: 2. Of those that a mesh axis runs over, the one named last changes fastest.
Arguments:
- in_factors: bfloat16 [2, 4, 512, 1024], P(None, ('parts', 'dp'), 'blk'), parts along dimension 1, may hold values from -6 to 6
- out_factors: bfloat16 [2, 4, 512, 1024], P(None, ('parts', 'dp'), 'blk'), parts along dimension 1, may hold values from -0.75 to 0.75
- lengths: int32 [4, 32], P(('parts', 'dp')), parts along dimension 0, may hold values from 1 to 64, 512 in all within a row
- signs: int32 [2, 1024, 1024], P(None, 'blk'), may hold values 0 or 1
- projection: bfloat16 [2, 1024, 16, 4096], P(None, 'blk', None, 'sub'), may hold values from -0.046875 to 0.046875
Outputs:
- features: float32 [4, 32, 2, 4096], P(('parts', 'dp'), 'blk', None, 'sub'), parts along dimension 0
The draws below stay inside these ranges and needn't reach their ends.
There are 2 independent parts, one for each index of `parts`. The reference program is written for one: setup_inputs(seed, part) draws one part's arguments, and reference() takes and returns one part's arrays. A program takes and returns all parts, laid end to end along the dimension named above; an argument that names none is the same for every part. Nothing has to cross between parts.
Inputs may be any that keep to these rules, and one draw needn't show every extreme that they name: In each row the 32 lengths sum to 512; the documents follow one another over the tokens of their dp index in order.
All inputs are finite; a program needn't handle non-finite values. No bound on the sum of `signs` on one device may be relied on, other than what follows from the above.
Results may differ from the reference program's by a relative error of at most 0.0029.
Values may be sent and summed in bfloat16 or wider, within the bound.
A program may use at most 128 MiB of HBM per device.

```python
import math
import jax
import jax.numpy as jnp
import numpy as np
from jax import lax

IN_DIM = 1024
OUT_DIM = 1024
PROJ = 4096
KEEP = 16
LAYERS = 2
EX_DEV = 32
TOK_DEV = 512
LEN_MAX = 64
N_DP = 2


def touch_ends(result, stream_key, smallest, largest):
    shape = result.shape
    spot = [jax.random.randint(jax.random.fold_in(stream_key, axis), (), 0, shape[axis]) for axis in range(len(shape))]
    result = result.at[tuple(spot)].set(smallest)
    longest = shape.index(max(shape))
    spot[longest] = (spot[longest] + 1) % shape[longest]
    return result.at[tuple(spot)].set(largest)


def level_of(rng, shape, cuts, least, high):
    gain, own = 1.0, jax.random.fold_in(rng, 6)
    for position, blocks in cuts:
        draws = jnp.exp(jax.random.uniform(jax.random.fold_in(own, position), (blocks,), jnp.float32, least / len(cuts), high / len(cuts)))
        gain = gain * jnp.repeat(draws, shape[position] // blocks).reshape([-1 if axis == position else 1 for axis in range(len(shape))])
    return gain


def split_up(count, total, most, skew):
    portions = [(1 << 20) // math.isqrt(grade ** skew) + 1 for grade in range(2, count + 1)]
    spare, holding = total - most - (count - 1), [1] * (count - 1)
    while spare > 0:
        free = [i for i in range(count - 1) if holding[i] < most]
        mass, remaining = sum([portions[i] for i in free]), spare
        for i in free:
            more = min(most - holding[i], max(1, remaining * portions[i] // mass), spare)
            holding[i] = holding[i] + more
            spare = spare - more
    return np.array([most] + holding)


def uneven(key, number_of, total, reach, slope):
    if number_of == 2:
        one = jax.random.randint(key, (), max(1, total - reach), min(reach, total - 1) + 1)
        return jnp.stack([one, total - one])
    tallies = jnp.asarray(split_up(number_of, total, reach, slope), jnp.int32)
    twos = (number_of - 1) // 2
    source_of, receiver = tallies[1:1 + 2 * twos:2], tallies[2:2 + 2 * twos:2]
    slack = jnp.minimum(source_of - 1, reach - receiver)
    moved = jax.random.randint(jax.random.fold_in(key, 1), (twos,), 0, 1 << 20) % (slack + 1)
    tallies = tallies.at[1:1 + 2 * twos:2].set(source_of - moved).at[2:2 + 2 * twos:2].set(receiver + moved)
    return tallies[jax.random.permutation(jax.random.fold_in(key, 2), number_of)]


def normal_values(key, shape, width, bound, pieces=(), kind=jnp.bfloat16):
    array = jax.random.normal(key, shape, jnp.float32) * width
    if len(pieces) > 0:
        array = level_of(key, shape, pieces, -0.22, 0.18) * array
    return jnp.clip(array, min=-bound, max=bound).astype(kind)


def setup_inputs(seed: int = 0, part: int = 0) -> dict:
    keys = jax.random.split(jax.random.key(seed), 6)
    part_splits = jax.random.split(jax.random.fold_in(keys[5], part), 6)
    return {
        "in_factors": normal_values(part_splits[0], (LAYERS, N_DP, TOK_DEV, IN_DIM), 1.0, 6.0, ((1, 2), (2, 4))),
        "out_factors": normal_values(part_splits[1], (LAYERS, N_DP, TOK_DEV, OUT_DIM), 0.125, 0.75, ((1, 2), (2, 4))),
        "lengths": jax.vmap(lambda own: uneven(own, EX_DEV, TOK_DEV, LEN_MAX, 2))(jax.random.split(part_splits[2], N_DP)).reshape((N_DP, EX_DEV)).astype(jnp.int32),
        "signs": touch_ends((jax.random.randint(keys[3], (LAYERS, IN_DIM, OUT_DIM), 0, 2) < 1).astype(jnp.int32), jax.random.fold_in(keys[3], 1), 0, 1),
        "projection": normal_values(keys[4], (LAYERS, IN_DIM, KEEP, PROJ), (IN_DIM * KEEP) ** -0.5, 0.046875, ((1, 4), (3, 2))),
    }


def parity_sign(values):
    total = jnp.zeros_like(values)
    for bit_level in range(16):
        total = total + jnp.bitwise_and(jnp.right_shift(values, bit_level), 1)
    return (1 - 2 * (total % 2)).astype(jnp.float32)

def parity_table(row_ids, col_ids):
    return parity_sign(jnp.bitwise_and(row_ids[:, None], col_ids[None, :]))

def reference(in_factors, out_factors, lengths, signs, projection):
    norm_scale = 1.0 / math.sqrt(IN_DIM * OUT_DIM)
    row_ids = jnp.arange(IN_DIM, dtype=jnp.int32)
    col_ids = jnp.arange(OUT_DIM, dtype=jnp.int32)
    kept_ids = jnp.arange(KEEP, dtype=jnp.int32)
    row_mix = parity_table(row_ids, row_ids)
    col_mix = parity_table(col_ids, kept_ids)
    window_ids = jnp.arange(LEN_MAX, dtype=jnp.int32)
    shards = []
    for dp_shard in range(N_DP):
        doc_lengths = lengths[dp_shard].astype(jnp.int32)
        doc_starts = (jnp.cumsum(doc_lengths) - doc_lengths).astype(jnp.int32)
        per_layer = []
        for layer_id in range(LAYERS):
            signed = (2 * signs[layer_id] - 1).astype(jnp.float32)
            mixing = signed[:, :, None] * col_mix[None, :, :]
            left_pad = jnp.pad(in_factors[layer_id, dp_shard].astype(jnp.float32), ((0, LEN_MAX), (0, 0)))
            right_pad = jnp.pad(out_factors[layer_id, dp_shard].astype(jnp.float32), ((0, LEN_MAX), (0, 0)))

            def one_example(bounds):
                offset, length = bounds
                left_window = lax.dynamic_slice_in_dim(left_pad, offset, LEN_MAX, 0)
                right_window = lax.dynamic_slice_in_dim(right_pad, offset, LEN_MAX, 0)
                inside = (window_ids < length)[:, None]
                left_window = jnp.where(inside, left_window, jnp.zeros_like(left_window))
                gradient = jnp.dot(left_window.T, right_window, precision=lax.Precision.HIGHEST)
                return jnp.einsum('ic,ick->ik', gradient, mixing, precision=lax.Precision.HIGHEST)
            folded = lax.map(one_example, (doc_starts, doc_lengths))
            transformed = jnp.einsum('ji,eik->ejk', row_mix, folded, precision=lax.Precision.HIGHEST) * norm_scale
            kept = transformed.astype(jnp.bfloat16).reshape(EX_DEV, IN_DIM * KEEP)
            weights = projection[layer_id].reshape(IN_DIM * KEEP, PROJ)
            per_layer.append(jnp.dot(kept, weights, preferred_element_type=jnp.float32))
        shards.append(jnp.stack(per_layer, axis=1))
    return jnp.stack(shards, axis=0)
```

```python
import functools
import math

import jax
import jax.numpy as jnp
from jax import lax
from jax.experimental import pallas as pl
from jax.experimental.pallas import tpu as pltpu
from jax.sharding import PartitionSpec as P

MESH = pl.DeviceIdType.MESH


def swapped(block, axis, bit):
    count = lax.axis_size(axis)
    route = []
    for low in range(count):
        high = low | 1 << bit
        if high != low and high < count:
            route += [(low, high), (high, low)]
    return lax.ppermute(block, axis, route)


def parity_sign(values):
    total = jnp.zeros_like(values)
    for bit_level in range(16):
        total = total + jnp.bitwise_and(jnp.right_shift(values, bit_level), 1)
    return (1 - 2 * (total % 2)).astype(jnp.float32)


def parity_table(row_ids, col_ids):
    return parity_sign(jnp.bitwise_and(row_ids[:, None], col_ids[None, :]))


def build_weighted(owners, example_ids, input_cols):
    one_hot = (owners[:, None] == example_ids[None, :]).astype(jnp.bfloat16)
    product = one_hot[None, :, :, None] * input_cols[:, 0, :, None, :]
    return product.reshape(product.shape[0], product.shape[1], product.shape[2] * product.shape[3])


def make_accumulate(weighted, portion):
    return jnp.einsum("ltx,ltc->lxc", weighted, portion[:, 0], preferred_element_type=jnp.float32)


def shards(in_factors, out_factors, lengths, signs, projection):
    blocks = lax.axis_size("blk")
    halves = lax.axis_size("sub")
    my_block = lax.axis_index("blk")
    my_half = lax.axis_index("sub")
    layers = in_factors.shape[0]
    tok_local = in_factors.shape[2]
    in_width = in_factors.shape[3]
    out_width = out_factors.shape[3]
    rows_block = in_width // blocks
    documents = lengths.shape[1]
    kept_cols = projection.shape[2]
    tok_shard = tok_local * blocks
    norm_scale = 1.0 / math.sqrt(in_width * out_width)
    input_cols = lax.all_to_all(in_factors, "blk", split_axis=3, concat_axis=2, tiled=True)
    doc_ends = jnp.cumsum(lengths[0])
    positions = jnp.arange(tok_shard, dtype=jnp.int32)
    owners = jnp.sum((positions[:, None] >= doc_ends[None, :]).astype(jnp.int32), axis=1)
    width_part = out_width // halves
    col_base = my_half * width_part
    example_ids = jnp.arange(documents, dtype=jnp.int32)
    right_part = lax.dynamic_slice_in_dim(out_factors, col_base, width_part, 3)
    weighted = build_weighted(owners, example_ids, input_cols)
    gradients = make_accumulate(weighted, lax.all_gather(right_part, "blk", axis=2, tiled=True))
    gradients = gradients.reshape(layers, documents, rows_block, width_part)
    col_ids = col_base + jnp.arange(width_part, dtype=jnp.int32)
    sign_slice = lax.dynamic_slice_in_dim(signs, col_base, width_part, 2)
    signed = (2 * sign_slice - 1).astype(jnp.float32)
    col_mix = parity_table(col_ids, jnp.arange(kept_cols, dtype=jnp.int32))
    mixing = signed[:, :, :, None] * col_mix[None, None, :, :]
    folded = jnp.einsum("leic,lick->leik", gradients, mixing, precision=lax.Precision.HIGHEST)
    local_rows = jnp.arange(rows_block, dtype=jnp.int32)
    row_mix = parity_table(local_rows, local_rows)
    within = jnp.einsum("ji,leik->lejk", row_mix, folded, precision=lax.Precision.HIGHEST)
    within = within.reshape(layers, documents, rows_block * kept_cols)
    within = lax.psum_scatter(within, "sub", scatter_dimension=1, tiled=True)
    blended = within
    for bit_level in range(blocks.bit_length() - 1):
        partner = swapped(blended, "blk", bit_level)
        high_bit = jnp.bitwise_and(jnp.right_shift(my_block, bit_level), 1)
        blended = partner + (1 - 2 * high_bit).astype(jnp.float32) * blended
    kept_half = (blended * norm_scale).astype(jnp.bfloat16)
    gathered = lax.all_gather(kept_half, "sub", axis=1, tiled=True)
    weights = projection.reshape(layers, rows_block * kept_cols, projection.shape[3])
    features = lax.psum_scatter(
        jnp.einsum("lek,lkp->elp", gathered, weights, preferred_element_type=jnp.float32),
        "blk",
        scatter_dimension=0,
        tiled=True,
    )
    return features[None]


def parity(values):
    for shift in (8, 4, 2, 1):
        values = jnp.bitwise_xor(values, jnp.right_shift(values, shift))
    return jnp.bitwise_and(values, 1)


def pm_one(values):
    return (1 - 2 * parity(values)).astype(jnp.float32)


def iota(shape, axis):
    return lax.broadcasted_iota(jnp.int32, shape, axis)


def split_terms(value, terms):
    parts = []
    for _ in range(terms):
        part = value.astype(jnp.bfloat16)
        parts.append(part)
        value = value - part.astype(jnp.float32)
    return parts


def dot(a, b):
    return jnp.dot(a, b, preferred_element_type=jnp.float32)


def sketch_kernel(dims, len_ref, in_ref, out_ref, signs_ref, proj_ref, feat_ref,
                  in_all, out_all, sign_buf, sign_t, had, perm, weights, folded, stage_own, stage_rx,
                  kept, own_feat, feat_tx, feat_rx,
                  proj_sem, sign_sem, out_recv, out_send, in_recv, in_send,
                  st_send, st_recv, kept_sem, ft_send, ft_recv):
    n, halves, layers, tok, width, cols, rows, docs, kc, feats, scale = dims
    me = lax.axis_index("blk")
    half = lax.axis_index("sub")
    other = 1 - half
    layer = half
    stages = n.bit_length() - 1
    pieces = stage_own.shape[1]
    kper = kc // pieces
    mine = docs // n
    gl = perm.shape[0]
    jl = gl // kc
    groups = rows // jl
    kdim = rows * kc
    hq = feats // 2

    slabs = proj_sem.shape[1]
    depth = kdim // slabs

    def slab(which, piece):
        at = pl.ds(piece * depth, depth)
        return pltpu.make_async_copy(proj_ref.at[which, at], weights.at[which, at], proj_sem.at[which, piece])

    own_out = pltpu.make_async_copy(out_ref.at[layer, 0], out_all.at[me], out_recv.at[me])
    own_in = pltpu.make_async_copy(in_ref.at[layer, 0, :, pl.ds(pl.multiple_of(me * rows, 128), rows)], in_all.at[me], in_recv.at[me])
    own_sign = pltpu.make_async_copy(signs_ref.at[layer], sign_buf, sign_sem)
    own_sign.start()
    own_out.start()
    own_in.start()

    barrier = pltpu.get_barrier_semaphore()
    for step in range(1, n):
        pl.semaphore_signal(barrier, inc=1, device_id={"blk": lax.rem(me + step, n)}, device_id_type=MESH)
    pl.semaphore_signal(barrier, inc=1, device_id={"sub": other}, device_id_type=MESH)
    pl.semaphore_wait(barrier, n)

    def out_copy(src, shard, direction):
        return pltpu.make_async_remote_copy(
            src_ref=src, dst_ref=out_all.at[shard], send_sem=out_send.at[direction, shard], recv_sem=out_recv.at[shard],
            device_id={"blk": me + 1 - 2 * direction}, device_id_type=MESH)

    def in_copy(step):
        to = lax.rem(me + step, n)
        return pltpu.make_async_remote_copy(
            src_ref=in_ref.at[layer, 0, :, pl.ds(pl.multiple_of(to * rows, 128), rows)], dst_ref=in_all.at[me],
            send_sem=in_send.at[to], recv_sem=in_recv.at[me], device_id={"blk": to}, device_id_type=MESH)

    @pl.when(me < n - 1)
    def _():
        out_copy(out_ref.at[layer, 0], me, 0).start()

    @pl.when(me > 0)
    def _():
        out_copy(out_ref.at[layer, 0], me, 1).start()

    for step in sorted(range(1, n), key=lambda s: min(s, n - s)):
        in_copy(step).start()

    for which in range(layers):
        for piece in range(slabs):
            slab(which, piece).start()

    had[...] = pm_one(jnp.bitwise_and(iota((rows, rows), 0), iota((rows, rows), 1))).astype(jnp.bfloat16)
    source, target = iota((gl, gl), 0), iota((gl, gl), 1)
    perm[...] = jnp.where((source % jl) * kc + source // jl == target, 1.0, 0.0).astype(jnp.bfloat16)
    spread = jnp.broadcast_to(len_ref[...], (docs, docs)).astype(jnp.float32)
    row_id, col_id = iota((docs, docs), 0), iota((docs, docs), 1)
    first = jnp.sum(jnp.where(col_id < row_id, spread, 0.0), axis=1, keepdims=True)
    last = jnp.sum(jnp.where(col_id <= row_id, spread, 0.0), axis=1, keepdims=True)
    folded[...] = jnp.zeros_like(folded)
    own_sign.wait()
    sign_t[...] = (2 * sign_buf[...] - 1).astype(jnp.float32).T.astype(jnp.bfloat16)

    def visit(turn, carry):
        step = turn // 2
        shard = me + step * (1 - 2 * (turn % 2))

        @pl.when(jnp.logical_and(jnp.logical_and(shard >= 0, shard < n), turn != 1))
        def _():
            pltpu.make_async_copy(out_all.at[shard], out_all.at[shard], out_recv.at[shard]).wait()

            @pl.when(jnp.logical_and(shard < me, me < n - 1))
            def _():
                out_copy(out_all.at[shard], shard, 0).start()

            @pl.when(jnp.logical_and(shard > me, me > 0))
            def _():
                out_copy(out_all.at[shard], shard, 1).start()

            pltpu.make_async_copy(in_all.at[shard], in_all.at[shard], in_recv.at[shard]).wait()
            position = (iota((docs, tok), 1) + shard * tok).astype(jnp.float32)
            hot = jnp.where(jnp.logical_and(position >= first, position < last), 1.0, 0.0).astype(jnp.bfloat16)
            hot = jnp.concatenate([hot, hot], axis=1)

            def some(group, carry):
                right = out_all[shard]
                left = in_all[shard].astype(jnp.float32)
                col_ids = iota((1, cols), 1)
                signed = [
                    right * pm_one(jnp.bitwise_and(col_ids, group * kper + at)).astype(jnp.bfloat16) for at in range(kper)
                ]
                product = dot(jnp.concatenate(signed, axis=0), sign_t[...])
                for at in range(kper):
                    terms = split_terms(product[at * tok:(at + 1) * tok] * left, 2)
                    where = pl.ds(pl.multiple_of((group * kper + at) * docs, docs), docs)
                    folded[where, :] += dot(hot, jnp.concatenate(terms, axis=0))
                return carry

            lax.fori_loop(0, pieces, some, 0)

        return carry

    lax.fori_loop(0, 2 * n, visit, 0)

    def stage_copy(stage, piece):
        bit = 1 << stage
        partner = me + bit * (1 - 2 * ((me // bit) % 2))
        return pltpu.make_async_remote_copy(
            src_ref=stage_own.at[stage, piece], dst_ref=stage_rx.at[stage, piece],
            send_sem=st_send.at[stage, piece], recv_sem=st_recv.at[stage, piece],
            device_id={"blk": partner}, device_id_type=MESH)

    span = kper * docs
    for piece in range(pieces):
        total = None
        for term in split_terms(folded[piece * span:(piece + 1) * span, :], 3):
            value = dot(term, had[...])
            total = value if total is None else total + value
        stage_own[0, piece] = total
        stage_copy(0, piece).start()
    for stage in range(stages):
        keep_sign = (1 - 2 * ((me // (1 << stage)) % 2)).astype(jnp.float32)
        for piece in range(pieces):
            stage_copy(stage, piece).wait_recv()
            value = stage_rx[stage, piece] + keep_sign * stage_own[stage, piece]
            if stage < stages - 1:
                stage_own[stage + 1, piece] = value
                stage_copy(stage + 1, piece).start()
            else:
                value = (value * scale).astype(jnp.bfloat16).astype(jnp.float32)
                folded[piece * span:(piece + 1) * span, :] = value

    kl = 128 // jl
    lane = iota((docs, 128), 1) // jl
    for group in range(groups):
        tiles = []
        for part in range(gl // 128):
            tile = None
            for at in range(kl):
                k = part * kl + at
                place = group * jl
                base = place // 128 * 128
                piece = folded[k * docs:(k + 1) * docs, base:base + 128]
                shift = (at * jl - (place - base)) % 128
                if shift:
                    piece = pltpu.roll(piece, shift, 1)
                tile = piece if tile is None else jnp.where(lane == at, piece, tile)
            tiles.append(tile)
        line = jnp.concatenate(tiles, axis=1).astype(jnp.bfloat16)
        kept[half, group * docs:(group + 1) * docs, :] = dot(line, perm[...]).astype(jnp.bfloat16)
    kept_copy = pltpu.make_async_remote_copy(
        src_ref=kept.at[half], dst_ref=kept.at[half], send_sem=kept_sem.at[0], recv_sem=kept_sem.at[1],
        device_id={"sub": other}, device_id_type=MESH)
    kept_copy.start()

    def feat_copy(which, step):
        to = lax.rem(me + step, n)
        return pltpu.make_async_remote_copy(
            src_ref=feat_tx.at[which, to], dst_ref=feat_rx.at[which, me],
            send_sem=ft_send.at[which, to], recv_sem=ft_recv.at[which, me],
            device_id={"blk": to}, device_id_type=MESH)

    def feat_arrived(which, step):
        source = lax.rem(me + step, n)
        return pltpu.make_async_copy(feat_rx.at[which, source], feat_rx.at[which, source], ft_recv.at[which, source])

    per = depth // gl
    for turn in range(2):
        which = half if turn == 0 else other
        if turn == 1:
            kept_copy.wait_recv()
        own_feat[which] = jnp.zeros((docs, feats), jnp.float32)

        def slice_step(piece, carry):
            slab(which, piece).wait()
            lhs = jnp.concatenate(
                [kept[which, pl.ds(pl.multiple_of((piece * per + at) * docs, docs), docs), :] for at in range(per)], axis=1)
            own_feat[which] += dot(lhs, weights[which, pl.ds(pl.multiple_of(piece * depth, depth), depth), :])
            return carry

        lax.fori_loop(0, slabs, slice_step, 0)
        for owner in range(n):
            low = own_feat[which, owner * mine:(owner + 1) * mine, :hq]
            high = own_feat[which, owner * mine:(owner + 1) * mine, hq:]
            feat_tx[which, owner] = jnp.concatenate([low, high], axis=0).astype(jnp.bfloat16)
        for step in range(1, n):
            feat_copy(which, step).start()

    for turn in range(2):
        which = half if turn == 1 else other
        at = pl.ds(pl.multiple_of(me * mine, mine), mine)
        low = own_feat[which, at, :hq]
        high = own_feat[which, at, hq:]
        for step in range(1, n):
            feat_arrived(which, step).wait()
            block = feat_rx[which, lax.rem(me + step, n)].astype(jnp.float32)
            low = low + block[:mine]
            high = high + block[mine:]
        feat_ref[which, :, :hq] = low
        feat_ref[which, :, hq:] = high

    for shard in range(n):
        @pl.when(jnp.logical_and(shard <= me, me < n - 1))
        def _():
            out_copy(out_all.at[shard], shard, 0).wait_send()

        @pl.when(jnp.logical_and(shard >= me, me > 0))
        def _():
            out_copy(out_all.at[shard], shard, 1).wait_send()

    for step in range(1, n):
        in_copy(step).wait_send()
        for which in range(2):
            feat_copy(which, step).wait_send()
    for stage in range(stages):
        for piece in range(pieces):
            stage_copy(stage, piece).wait_send()
    kept_copy.wait_send()


def sketch(in_factors, out_factors, lengths, signs, projection):
    n = lax.axis_size("blk")
    halves = lax.axis_size("sub")
    layers, _, tok, width = in_factors.shape
    cols = out_factors.shape[3]
    rows = signs.shape[1]
    docs = lengths.shape[1]
    kc = projection.shape[2]
    feats = projection.shape[3]
    scale = 1.0 / math.sqrt(width * cols)
    dims = (n, halves, layers, tok, width, cols, rows, docs, kc, feats, scale)
    stages = n.bit_length() - 1
    pieces, slabs, gl = 4, 4, 256
    kdim = rows * kc
    bf16, f32, dma = jnp.bfloat16, jnp.float32, pltpu.SemaphoreType.DMA
    anywhere = pl.BlockSpec(memory_space=pl.ANY)
    vmem = pl.BlockSpec(memory_space=pltpu.VMEM)
    features = pl.pallas_call(
        functools.partial(sketch_kernel, dims),
        out_shape=jax.ShapeDtypeStruct((layers, docs // n, feats), f32),
        in_specs=[vmem, anywhere, anywhere, anywhere, anywhere],
        out_specs=vmem,
        scratch_shapes=[
            pltpu.VMEM((n, tok, rows), bf16),
            pltpu.VMEM((n, tok, cols), bf16),
            pltpu.VMEM((rows, cols), jnp.int32),
            pltpu.VMEM((cols, rows), bf16),
            pltpu.VMEM((rows, rows), bf16),
            pltpu.VMEM((gl, gl), bf16),
            pltpu.VMEM((layers, kdim, feats), bf16),
            pltpu.VMEM((kc * docs, rows), f32),
            pltpu.VMEM((stages, pieces, kc // pieces * docs, rows), f32),
            pltpu.VMEM((stages, pieces, kc // pieces * docs, rows), f32),
            pltpu.VMEM((layers, kdim // gl * docs, gl), bf16),
            pltpu.VMEM((layers, docs, feats), f32),
            pltpu.VMEM((layers, n, 2 * docs // n, feats // 2), bf16),
            pltpu.VMEM((layers, n, 2 * docs // n, feats // 2), bf16),
            dma((layers, slabs)), dma, dma((n,)), dma((2, n)), dma((n,)), dma((n,)),
            dma((stages, pieces)), dma((stages, pieces)), dma((2,)), dma((layers, n)), dma((layers, n)),
        ],
        compiler_params=pltpu.CompilerParams(collective_id=0, has_side_effects=True, vmem_limit_bytes=56 << 20),
    )(lengths, in_factors, out_factors, signs, projection.reshape(layers, kdim, feats))
    return jnp.transpose(features, (1, 0, 2))[None]


def pick(in_factors, out_factors, lengths, signs, projection):
    n = lax.axis_size("blk")
    layers, _, tok, width = in_factors.shape
    fits = (
        n > 1 and n & (n - 1) == 0
        and layers == 2 and lax.axis_size("sub") == 2
        and signs.shape[1] % 256 == 0 and tok % 128 == 0
        and lengths.shape[1] % (8 * n) == 0 and 128 % projection.shape[2] == 0 and projection.shape[2] % 16 == 0
        and projection.shape[3] % 256 == 0
        and projection.size * projection.dtype.itemsize <= 36 << 20
    )
    run = sketch if fits else shards
    return run(in_factors, out_factors, lengths, signs, projection)


def solution(mesh):
    return jax.shard_map(
        pick,
        mesh=mesh,
        in_specs=(
            P(None, ("parts", "dp"), "blk", None),
            P(None, ("parts", "dp"), "blk", None),
            P(("parts", "dp"), None),
            P(None, "blk", None),
            P(None, "blk", None, "sub"),
        ),
        out_specs=P(("parts", "dp"), "blk", None, "sub"),
        check_vma=False,
    )
```

```python
import functools
import math

import jax
import jax.numpy as jnp
from jax import lax
from jax.experimental import pallas as pl
from jax.experimental.pallas import tpu as pltpu
from jax.sharding import PartitionSpec as P

MESH = pl.DeviceIdType.MESH


def swapped(block, axis, bit):
    count = lax.axis_size(axis)
    route = []
    for low in range(count):
        high = low | 1 << bit
        if high != low and high < count:
            route += [(low, high), (high, low)]
    return lax.ppermute(block, axis, route)


def parity_sign(values):
    total = jnp.zeros_like(values)
    for bit_level in range(16):
        total = total + jnp.bitwise_and(jnp.right_shift(values, bit_level), 1)
    return (1 - 2 * (total % 2)).astype(jnp.float32)


def parity_table(row_ids, col_ids):
    return parity_sign(jnp.bitwise_and(row_ids[:, None], col_ids[None, :]))


def build_weighted(owners, example_ids, input_cols):
    one_hot = (owners[:, None] == example_ids[None, :]).astype(jnp.bfloat16)
    product = one_hot[None, :, :, None] * input_cols[:, 0, :, None, :]
    return product.reshape(product.shape[0], product.shape[1], product.shape[2] * product.shape[3])


def make_accumulate(weighted, portion):
    return jnp.einsum("ltx,ltc->lxc", weighted, portion[:, 0], preferred_element_type=jnp.float32)


def shards(in_factors, out_factors, lengths, signs, projection):
    blocks = lax.axis_size("blk")
    halves = lax.axis_size("sub")
    my_block = lax.axis_index("blk")
    my_half = lax.axis_index("sub")
    layers = in_factors.shape[0]
    tok_local = in_factors.shape[2]
    in_width = in_factors.shape[3]
    out_width = out_factors.shape[3]
    rows_block = in_width // blocks
    documents = lengths.shape[1]
    kept_cols = projection.shape[2]
    tok_shard = tok_local * blocks
    norm_scale = 1.0 / math.sqrt(in_width * out_width)
    input_cols = lax.all_to_all(in_factors, "blk", split_axis=3, concat_axis=2, tiled=True)
    doc_ends = jnp.cumsum(lengths[0])
    positions = jnp.arange(tok_shard, dtype=jnp.int32)
    owners = jnp.sum((positions[:, None] >= doc_ends[None, :]).astype(jnp.int32), axis=1)
    width_part = out_width // halves
    col_base = my_half * width_part
    example_ids = jnp.arange(documents, dtype=jnp.int32)
    right_part = lax.dynamic_slice_in_dim(out_factors, col_base, width_part, 3)
    weighted = build_weighted(owners, example_ids, input_cols)
    gradients = make_accumulate(weighted, lax.all_gather(right_part, "blk", axis=2, tiled=True))
    gradients = gradients.reshape(layers, documents, rows_block, width_part)
    col_ids = col_base + jnp.arange(width_part, dtype=jnp.int32)
    sign_slice = lax.dynamic_slice_in_dim(signs, col_base, width_part, 2)
    signed = (2 * sign_slice - 1).astype(jnp.float32)
    col_mix = parity_table(col_ids, jnp.arange(kept_cols, dtype=jnp.int32))
    mixing = signed[:, :, :, None] * col_mix[None, None, :, :]
    folded = jnp.einsum("leic,lick->leik", gradients, mixing, precision=lax.Precision.HIGHEST)
    local_rows = jnp.arange(rows_block, dtype=jnp.int32)
    row_mix = parity_table(local_rows, local_rows)
    within = jnp.einsum("ji,leik->lejk", row_mix, folded, precision=lax.Precision.HIGHEST)
    within = within.reshape(layers, documents, rows_block * kept_cols)
    within = lax.psum_scatter(within, "sub", scatter_dimension=1, tiled=True)
    blended = within
    for bit_level in range(blocks.bit_length() - 1):
        partner = swapped(blended, "blk", bit_level)
        high_bit = jnp.bitwise_and(jnp.right_shift(my_block, bit_level), 1)
        blended = partner + (1 - 2 * high_bit).astype(jnp.float32) * blended
    kept_half = (blended * norm_scale).astype(jnp.bfloat16)
    gathered = lax.all_gather(kept_half, "sub", axis=1, tiled=True)
    weights = projection.reshape(layers, rows_block * kept_cols, projection.shape[3])
    features = lax.psum_scatter(
        jnp.einsum("lek,lkp->elp", gathered, weights, preferred_element_type=jnp.float32),
        "blk",
        scatter_dimension=0,
        tiled=True,
    )
    return features[None]


def parity(values):
    for shift in (8, 4, 2, 1):
        values = jnp.bitwise_xor(values, jnp.right_shift(values, shift))
    return jnp.bitwise_and(values, 1)


def pm_one(values):
    return (1 - 2 * parity(values)).astype(jnp.float32)


def iota(shape, axis):
    return lax.broadcasted_iota(jnp.int32, shape, axis)


def split_terms(value, terms):
    parts = []
    for _ in range(terms):
        part = value.astype(jnp.bfloat16)
        parts.append(part)
        value = value - part.astype(jnp.float32)
    return parts


def dot(a, b):
    return jnp.dot(a, b, preferred_element_type=jnp.float32)


def sketch_kernel(dims, len_ref, in_ref, out_ref, signs_ref, proj_ref, feat_ref,
                  in_all, out_all, sign_buf, sign_t, had, perm, weights, folded, stage_own, stage_tx, stage_rx, stage_rx16,
                  kept, own_feat, feat_tx, feat_rx,
                  proj_sem, sign_sem, out_recv, out_send, in_recv, in_send,
                  st_send, st_recv, kept_sem, ft_send, ft_recv):
    n, halves, layers, tok, width, cols, rows, docs, kc, feats, scale = dims
    me = lax.axis_index("blk")
    half = lax.axis_index("sub")
    other = 1 - half
    layer = half
    stages = n.bit_length() - 1
    pieces = stage_own.shape[1]
    kper = 4
    wide = stage_rx.shape[1]
    mine = docs // n
    gl = perm.shape[0]
    jl = gl // kc
    groups = rows // jl
    kdim = rows * kc
    hq = feats // 2

    slabs = proj_sem.shape[1]
    depth = kdim // slabs

    def slab(which, piece):
        at = pl.ds(piece * depth, depth)
        return pltpu.make_async_copy(proj_ref.at[which, at], weights.at[which, at], proj_sem.at[which, piece])

    own_out = pltpu.make_async_copy(out_ref.at[layer, 0], out_all.at[me], out_recv.at[me])
    own_in = pltpu.make_async_copy(in_ref.at[layer, 0, :, pl.ds(pl.multiple_of(me * rows, 128), rows)], in_all.at[me], in_recv.at[me])
    own_sign = pltpu.make_async_copy(signs_ref.at[layer], sign_buf, sign_sem)
    own_sign.start()
    own_out.start()
    own_in.start()

    barrier = pltpu.get_barrier_semaphore()
    for step in range(1, n):
        pl.semaphore_signal(barrier, inc=1, device_id={"blk": lax.rem(me + step, n)}, device_id_type=MESH)
    pl.semaphore_signal(barrier, inc=1, device_id={"sub": other}, device_id_type=MESH)
    pl.semaphore_wait(barrier, n)

    def out_copy(src, shard, direction):
        return pltpu.make_async_remote_copy(
            src_ref=src, dst_ref=out_all.at[shard], send_sem=out_send.at[direction, shard], recv_sem=out_recv.at[shard],
            device_id={"blk": me + 1 - 2 * direction}, device_id_type=MESH)

    def in_copy(step):
        to = lax.rem(me + step, n)
        return pltpu.make_async_remote_copy(
            src_ref=in_ref.at[layer, 0, :, pl.ds(pl.multiple_of(to * rows, 128), rows)], dst_ref=in_all.at[me],
            send_sem=in_send.at[to], recv_sem=in_recv.at[me], device_id={"blk": to}, device_id_type=MESH)

    @pl.when(me < n - 1)
    def _():
        out_copy(out_ref.at[layer, 0], me, 0).start()

    @pl.when(me > 0)
    def _():
        out_copy(out_ref.at[layer, 0], me, 1).start()

    for step in sorted(range(1, n), key=lambda s: min(s, n - s)):
        in_copy(step).start()

    for which in range(layers):
        for piece in range(slabs):
            slab(which, piece).start()

    had[...] = pm_one(jnp.bitwise_and(iota((rows, rows), 0), iota((rows, rows), 1))).astype(jnp.bfloat16)
    source, target = iota((gl, gl), 0), iota((gl, gl), 1)
    perm[...] = jnp.where((source % jl) * kc + source // jl == target, 1.0, 0.0).astype(jnp.bfloat16)
    spread = jnp.broadcast_to(len_ref[...], (docs, docs)).astype(jnp.float32)
    row_id, col_id = iota((docs, docs), 0), iota((docs, docs), 1)
    first = jnp.sum(jnp.where(col_id < row_id, spread, 0.0), axis=1, keepdims=True)
    last = jnp.sum(jnp.where(col_id <= row_id, spread, 0.0), axis=1, keepdims=True)
    folded[...] = jnp.zeros_like(folded)
    own_sign.wait()
    sign_t[...] = (2 * sign_buf[...] - 1).astype(jnp.float32).T.astype(jnp.bfloat16)

    def visit(turn, carry):
        step = turn // 2
        shard = me + step * (1 - 2 * (turn % 2))

        @pl.when(jnp.logical_and(jnp.logical_and(shard >= 0, shard < n), turn != 1))
        def _():
            pltpu.make_async_copy(out_all.at[shard], out_all.at[shard], out_recv.at[shard]).wait()

            @pl.when(jnp.logical_and(shard < me, me < n - 1))
            def _():
                out_copy(out_all.at[shard], shard, 0).start()

            @pl.when(jnp.logical_and(shard > me, me > 0))
            def _():
                out_copy(out_all.at[shard], shard, 1).start()

            pltpu.make_async_copy(in_all.at[shard], in_all.at[shard], in_recv.at[shard]).wait()
            position = (iota((docs, tok), 1) + shard * tok).astype(jnp.float32)
            hot = jnp.where(jnp.logical_and(position >= first, position < last), 1.0, 0.0).astype(jnp.bfloat16)
            hot = jnp.concatenate([hot, hot], axis=1)

            def some(group, carry):
                right = out_all[shard]
                left = in_all[shard].astype(jnp.float32)
                col_ids = iota((1, cols), 1)
                signed = [
                    right * pm_one(jnp.bitwise_and(col_ids, group * kper + at)).astype(jnp.bfloat16) for at in range(kper)
                ]
                product = dot(jnp.concatenate(signed, axis=0), sign_t[...])
                for at in range(kper):
                    terms = split_terms(product[at * tok:(at + 1) * tok] * left, 2)
                    where = pl.ds(pl.multiple_of((group * kper + at) * docs, docs), docs)
                    folded[where, :] += dot(hot, jnp.concatenate(terms, axis=0))
                return carry

            lax.fori_loop(0, kc // kper, some, 0)

        return carry

    lax.fori_loop(0, 2 * n, visit, 0)

    def stage_copy(stage, piece):
        bit = 1 << stage
        partner = me + bit * (1 - 2 * ((me // bit) % 2))
        exact = piece < wide
        return pltpu.make_async_remote_copy(
            src_ref=stage_own.at[stage, piece] if exact else stage_tx.at[stage, piece - wide],
            dst_ref=stage_rx.at[stage, piece] if exact else stage_rx16.at[stage, piece - wide],
            send_sem=st_send.at[stage, piece], recv_sem=st_recv.at[stage, piece],
            device_id={"blk": partner}, device_id_type=MESH)

    def stage_send(stage, piece, value):
        stage_own[stage, piece] = value
        if piece >= wide:
            stage_tx[stage, piece - wide] = value.astype(jnp.bfloat16)
        stage_copy(stage, piece).start()

    def stage_take(stage, piece):
        stage_copy(stage, piece).wait_recv()
        if piece < wide:
            got = stage_rx[stage, piece]
        else:
            got = stage_rx16[stage, piece - wide].astype(jnp.float32)
        keep_sign = (1 - 2 * ((me // (1 << stage)) % 2)).astype(jnp.float32)
        return got + keep_sign * stage_own[stage, piece]

    ksplit = pieces // (rows // 128)
    span = kc // ksplit * docs

    def place(piece):
        return (slice(piece % ksplit * span, (piece % ksplit + 1) * span),
                slice(piece // ksplit * 128, (piece // ksplit + 1) * 128))

    for piece in range(pieces):
        total = None
        for term in split_terms(folded[place(piece)[0], :], 3):
            value = dot(term, had[:, place(piece)[1]])
            total = value if total is None else total + value
        stage_send(0, piece, total)
    for stage in range(stages - 1):
        for piece in range(pieces):
            stage_send(stage + 1, piece, stage_take(stage, piece))

    def feat_copy(which, step):
        to = lax.rem(me + step, n)
        return pltpu.make_async_remote_copy(
            src_ref=feat_tx.at[which, to], dst_ref=feat_rx.at[which, me],
            send_sem=ft_send.at[which, to], recv_sem=ft_recv.at[which, me],
            device_id={"blk": to}, device_id_type=MESH)

    def feat_arrived(which, step):
        source = lax.rem(me + step, n)
        return pltpu.make_async_copy(feat_rx.at[which, source], feat_rx.at[which, source], ft_recv.at[which, source])

    def kept_copy(part):
        lines = pl.ds(part * (128 // jl) * docs, 128 // jl * docs)
        return pltpu.make_async_remote_copy(
            src_ref=kept.at[half, lines], dst_ref=kept.at[half, lines],
            send_sem=kept_sem.at[0, part], recv_sem=kept_sem.at[1, part],
            device_id={"sub": other}, device_id_type=MESH)

    kl = 128 // jl
    lane = iota((docs, 128), 1) // jl
    per = depth // gl
    parts = rows // 128
    for row_part in range(parts):
        for piece in range(row_part * ksplit, (row_part + 1) * ksplit):
            folded[place(piece)] = (stage_take(stages - 1, piece) * scale).astype(jnp.bfloat16).astype(jnp.float32)
        base = row_part * 128
        for group in range(row_part * kl, (row_part + 1) * kl):
            tiles = []
            for part in range(gl // 128):
                tile = None
                for at in range(kl):
                    k = part * kl + at
                    piece = folded[k * docs:(k + 1) * docs, base:base + 128]
                    shift = (at * jl - (group * jl - base)) % 128
                    if shift:
                        piece = pltpu.roll(piece, shift, 1)
                    tile = piece if tile is None else jnp.where(lane == at, piece, tile)
                tiles.append(tile)
            line = jnp.concatenate(tiles, axis=1).astype(jnp.bfloat16)
            kept[half, group * docs:(group + 1) * docs, :] = dot(line, perm[...]).astype(jnp.bfloat16)
        kept_copy(row_part).start()

        for turn in range(2):
            which = half if turn == 0 else other
            if turn == 1:
                kept_copy(row_part).wait_recv()
            if row_part == 0:
                own_feat[which] = jnp.zeros((docs, feats), jnp.float32)

            def slice_step(piece, carry, which=which):
                slab(which, piece).wait()
                lhs = jnp.concatenate(
                    [kept[which, pl.ds(pl.multiple_of((piece * per + at) * docs, docs), docs), :] for at in range(per)],
                    axis=1)
                own_feat[which] += dot(lhs, weights[which, pl.ds(pl.multiple_of(piece * depth, depth), depth), :])
                return carry

            lax.fori_loop(row_part * (slabs // parts), (row_part + 1) * (slabs // parts), slice_step, 0)
            if row_part == parts - 1:
                for owner in range(n):
                    low = own_feat[which, owner * mine:(owner + 1) * mine, :hq]
                    high = own_feat[which, owner * mine:(owner + 1) * mine, hq:]
                    feat_tx[which, owner] = jnp.concatenate([low, high], axis=0).astype(jnp.bfloat16)
                for step in range(1, n):
                    feat_copy(which, step).start()

    for turn in range(2):
        which = half if turn == 1 else other
        at = pl.ds(pl.multiple_of(me * mine, mine), mine)
        low = own_feat[which, at, :hq]
        high = own_feat[which, at, hq:]
        for step in range(1, n):
            feat_arrived(which, step).wait()
            block = feat_rx[which, lax.rem(me + step, n)].astype(jnp.float32)
            low = low + block[:mine]
            high = high + block[mine:]
        feat_ref[which, :, :hq] = low
        feat_ref[which, :, hq:] = high

    for shard in range(n):
        @pl.when(jnp.logical_and(shard <= me, me < n - 1))
        def _():
            out_copy(out_all.at[shard], shard, 0).wait_send()

        @pl.when(jnp.logical_and(shard >= me, me > 0))
        def _():
            out_copy(out_all.at[shard], shard, 1).wait_send()

    for step in range(1, n):
        in_copy(step).wait_send()
        for which in range(2):
            feat_copy(which, step).wait_send()
    for stage in range(stages):
        for piece in range(pieces):
            stage_copy(stage, piece).wait_send()
    for part in range(parts):
        kept_copy(part).wait_send()


def sketch(in_factors, out_factors, lengths, signs, projection):
    n = lax.axis_size("blk")
    halves = lax.axis_size("sub")
    layers, _, tok, width = in_factors.shape
    cols = out_factors.shape[3]
    rows = signs.shape[1]
    docs = lengths.shape[1]
    kc = projection.shape[2]
    feats = projection.shape[3]
    scale = 1.0 / math.sqrt(width * cols)
    dims = (n, halves, layers, tok, width, cols, rows, docs, kc, feats, scale)
    stages = n.bit_length() - 1
    parts = rows // 128
    pieces, slabs, gl = 2 * parts, 2 * parts, 256
    wide = pieces // 2
    span = kc // 2 * docs
    kdim = rows * kc
    bf16, f32, dma = jnp.bfloat16, jnp.float32, pltpu.SemaphoreType.DMA
    anywhere = pl.BlockSpec(memory_space=pl.ANY)
    vmem = pl.BlockSpec(memory_space=pltpu.VMEM)
    features = pl.pallas_call(
        functools.partial(sketch_kernel, dims),
        out_shape=jax.ShapeDtypeStruct((layers, docs // n, feats), f32),
        in_specs=[vmem, anywhere, anywhere, anywhere, anywhere],
        out_specs=vmem,
        scratch_shapes=[
            pltpu.VMEM((n, tok, rows), bf16),
            pltpu.VMEM((n, tok, cols), bf16),
            pltpu.VMEM((rows, cols), jnp.int32),
            pltpu.VMEM((cols, rows), bf16),
            pltpu.VMEM((rows, rows), bf16),
            pltpu.VMEM((gl, gl), bf16),
            pltpu.VMEM((layers, kdim, feats), bf16),
            pltpu.VMEM((kc * docs, rows), f32),
            pltpu.VMEM((stages, pieces, span, 128), f32),
            pltpu.VMEM((stages, pieces - wide, span, 128), bf16),
            pltpu.VMEM((stages, wide, span, 128), f32),
            pltpu.VMEM((stages, pieces - wide, span, 128), bf16),
            pltpu.VMEM((layers, kdim // gl * docs, gl), bf16),
            pltpu.VMEM((layers, docs, feats), f32),
            pltpu.VMEM((layers, n, 2 * docs // n, feats // 2), bf16),
            pltpu.VMEM((layers, n, 2 * docs // n, feats // 2), bf16),
            dma((layers, slabs)), dma, dma((n,)), dma((2, n)), dma((n,)), dma((n,)),
            dma((stages, pieces)), dma((stages, pieces)), dma((2, parts)), dma((layers, n)), dma((layers, n)),
        ],
        compiler_params=pltpu.CompilerParams(collective_id=0, has_side_effects=True, vmem_limit_bytes=56 << 20),
    )(lengths, in_factors, out_factors, signs, projection.reshape(layers, kdim, feats))
    return jnp.transpose(features, (1, 0, 2))[None]


def pick(in_factors, out_factors, lengths, signs, projection):
    n = lax.axis_size("blk")
    layers, _, tok, width = in_factors.shape
    fits = (
        n > 1 and n & (n - 1) == 0
        and layers == 2 and lax.axis_size("sub") == 2
        and signs.shape[1] % 256 == 0 and tok % 128 == 0
        and lengths.shape[1] % (8 * n) == 0 and projection.shape[2] == 16
        and projection.shape[3] % 256 == 0
        and projection.size * projection.dtype.itemsize <= 36 << 20
    )
    run = sketch if fits else shards
    return run(in_factors, out_factors, lengths, signs, projection)


def solution(mesh):
    return jax.shard_map(
        pick,
        mesh=mesh,
        in_specs=(
            P(None, ("parts", "dp"), "blk", None),
            P(None, ("parts", "dp"), "blk", None),
            P(("parts", "dp"), None),
            P(None, "blk", None),
            P(None, "blk", None, "sub"),
        ),
        out_specs=P(("parts", "dp"), "blk", None, "sub"),
        check_vma=False,
    )
```

```python
import functools
import math

import jax
import jax.numpy as jnp
from jax import lax
from jax.experimental import pallas as pl
from jax.experimental.pallas import tpu as pltpu
from jax.sharding import PartitionSpec as P

MESH = pl.DeviceIdType.MESH


def swapped(block, axis, bit):
    count = lax.axis_size(axis)
    route = []
    for low in range(count):
        high = low | 1 << bit
        if high != low and high < count:
            route += [(low, high), (high, low)]
    return lax.ppermute(block, axis, route)


def parity_sign(values):
    total = jnp.zeros_like(values)
    for bit_level in range(16):
        total = total + jnp.bitwise_and(jnp.right_shift(values, bit_level), 1)
    return (1 - 2 * (total % 2)).astype(jnp.float32)


def parity_table(row_ids, col_ids):
    return parity_sign(jnp.bitwise_and(row_ids[:, None], col_ids[None, :]))


def build_weighted(owners, example_ids, input_cols):
    one_hot = (owners[:, None] == example_ids[None, :]).astype(jnp.bfloat16)
    product = one_hot[None, :, :, None] * input_cols[:, 0, :, None, :]
    return product.reshape(product.shape[0], product.shape[1], product.shape[2] * product.shape[3])


def make_accumulate(weighted, portion):
    return jnp.einsum("ltx,ltc->lxc", weighted, portion[:, 0], preferred_element_type=jnp.float32)


def shards(in_factors, out_factors, lengths, signs, projection):
    blocks = lax.axis_size("blk")
    halves = lax.axis_size("sub")
    my_block = lax.axis_index("blk")
    my_half = lax.axis_index("sub")
    layers = in_factors.shape[0]
    tok_local = in_factors.shape[2]
    in_width = in_factors.shape[3]
    out_width = out_factors.shape[3]
    rows_block = in_width // blocks
    documents = lengths.shape[1]
    kept_cols = projection.shape[2]
    tok_shard = tok_local * blocks
    norm_scale = 1.0 / math.sqrt(in_width * out_width)
    input_cols = lax.all_to_all(in_factors, "blk", split_axis=3, concat_axis=2, tiled=True)
    doc_ends = jnp.cumsum(lengths[0])
    positions = jnp.arange(tok_shard, dtype=jnp.int32)
    owners = jnp.sum((positions[:, None] >= doc_ends[None, :]).astype(jnp.int32), axis=1)
    width_part = out_width // halves
    col_base = my_half * width_part
    example_ids = jnp.arange(documents, dtype=jnp.int32)
    right_part = lax.dynamic_slice_in_dim(out_factors, col_base, width_part, 3)
    weighted = build_weighted(owners, example_ids, input_cols)
    gradients = make_accumulate(weighted, lax.all_gather(right_part, "blk", axis=2, tiled=True))
    gradients = gradients.reshape(layers, documents, rows_block, width_part)
    col_ids = col_base + jnp.arange(width_part, dtype=jnp.int32)
    sign_slice = lax.dynamic_slice_in_dim(signs, col_base, width_part, 2)
    signed = (2 * sign_slice - 1).astype(jnp.float32)
    col_mix = parity_table(col_ids, jnp.arange(kept_cols, dtype=jnp.int32))
    mixing = signed[:, :, :, None] * col_mix[None, None, :, :]
    folded = jnp.einsum("leic,lick->leik", gradients, mixing, precision=lax.Precision.HIGHEST)
    local_rows = jnp.arange(rows_block, dtype=jnp.int32)
    row_mix = parity_table(local_rows, local_rows)
    within = jnp.einsum("ji,leik->lejk", row_mix, folded, precision=lax.Precision.HIGHEST)
    within = within.reshape(layers, documents, rows_block * kept_cols)
    within = lax.psum_scatter(within, "sub", scatter_dimension=1, tiled=True)
    blended = within
    for bit_level in range(blocks.bit_length() - 1):
        partner = swapped(blended, "blk", bit_level)
        high_bit = jnp.bitwise_and(jnp.right_shift(my_block, bit_level), 1)
        blended = partner + (1 - 2 * high_bit).astype(jnp.float32) * blended
    kept_half = (blended * norm_scale).astype(jnp.bfloat16)
    gathered = lax.all_gather(kept_half, "sub", axis=1, tiled=True)
    weights = projection.reshape(layers, rows_block * kept_cols, projection.shape[3])
    features = lax.psum_scatter(
        jnp.einsum("lek,lkp->elp", gathered, weights, preferred_element_type=jnp.float32),
        "blk",
        scatter_dimension=0,
        tiled=True,
    )
    return features[None]


def parity(values):
    for shift in (8, 4, 2, 1):
        values = jnp.bitwise_xor(values, jnp.right_shift(values, shift))
    return jnp.bitwise_and(values, 1)


def pm_one(values):
    return (1 - 2 * parity(values)).astype(jnp.float32)


def iota(shape, axis):
    return lax.broadcasted_iota(jnp.int32, shape, axis)


def split_terms(value, terms):
    parts = []
    for _ in range(terms):
        part = value.astype(jnp.bfloat16)
        parts.append(part)
        value = value - part.astype(jnp.float32)
    return parts


def dot(a, b):
    return jnp.dot(a, b, preferred_element_type=jnp.float32)


def sketch_kernel(dims, len_ref, in_ref, out_ref, signs_ref, proj_ref, feat_ref,
                  in_all, out_all, sign_buf, sign_t, had, perm, weights, folded, stage_own, stage_tx, stage_rx, stage_rx16,
                  kept, own_feat, feat_tx, feat_rx,
                  proj_sem, sign_sem, out_recv, out_send, in_recv, in_send,
                  st_send, st_recv, kept_sem, ft_send, ft_recv):
    n, halves, layers, tok, width, cols, rows, docs, kc, feats, scale = dims
    me = lax.axis_index("blk")
    half = lax.axis_index("sub")
    other = 1 - half
    layer = half
    stages = n.bit_length() - 1
    pieces = stage_own.shape[1]
    kper = 4
    wide = stage_rx.shape[1]
    mine = docs // n
    gl = perm.shape[0]
    jl = gl // kc
    groups = rows // jl
    kdim = rows * kc
    cuts = feat_tx.shape[1]
    hq = feats // cuts // 2

    slabs = proj_sem.shape[1]
    depth = kdim // slabs

    def slab(which, piece):
        at = pl.ds(piece * depth, depth)
        return pltpu.make_async_copy(proj_ref.at[which, at], weights.at[which, at], proj_sem.at[which, piece])

    own_out = pltpu.make_async_copy(out_ref.at[layer, 0], out_all.at[me], out_recv.at[me])
    own_in = pltpu.make_async_copy(in_ref.at[layer, 0, :, pl.ds(pl.multiple_of(me * rows, 128), rows)], in_all.at[me], in_recv.at[me])
    own_sign = pltpu.make_async_copy(signs_ref.at[layer], sign_buf, sign_sem)
    own_sign.start()
    own_out.start()
    own_in.start()

    barrier = pltpu.get_barrier_semaphore()
    for step in range(1, n):
        pl.semaphore_signal(barrier, inc=1, device_id={"blk": lax.rem(me + step, n)}, device_id_type=MESH)
    pl.semaphore_signal(barrier, inc=1, device_id={"sub": other}, device_id_type=MESH)
    pl.semaphore_wait(barrier, n)

    def out_copy(src, shard, direction):
        return pltpu.make_async_remote_copy(
            src_ref=src, dst_ref=out_all.at[shard], send_sem=out_send.at[direction, shard], recv_sem=out_recv.at[shard],
            device_id={"blk": me + 1 - 2 * direction}, device_id_type=MESH)

    def in_copy(step):
        to = lax.rem(me + step, n)
        return pltpu.make_async_remote_copy(
            src_ref=in_ref.at[layer, 0, :, pl.ds(pl.multiple_of(to * rows, 128), rows)], dst_ref=in_all.at[me],
            send_sem=in_send.at[to], recv_sem=in_recv.at[me], device_id={"blk": to}, device_id_type=MESH)

    @pl.when(me < n - 1)
    def _():
        out_copy(out_ref.at[layer, 0], me, 0).start()

    @pl.when(me > 0)
    def _():
        out_copy(out_ref.at[layer, 0], me, 1).start()

    for step in sorted(range(1, n), key=lambda s: min(s, n - s)):
        in_copy(step).start()

    for which in range(layers):
        for piece in range(slabs):
            slab(which, piece).start()

    had[...] = pm_one(jnp.bitwise_and(iota((rows, rows), 0), iota((rows, rows), 1))).astype(jnp.bfloat16)
    source, target = iota((gl, gl), 0), iota((gl, gl), 1)
    perm[...] = jnp.where((source % jl) * kc + source // jl == target, 1.0, 0.0).astype(jnp.bfloat16)
    spread = jnp.broadcast_to(len_ref[...], (docs, docs)).astype(jnp.float32)
    row_id, col_id = iota((docs, docs), 0), iota((docs, docs), 1)
    first = jnp.sum(jnp.where(col_id < row_id, spread, 0.0), axis=1, keepdims=True)
    last = jnp.sum(jnp.where(col_id <= row_id, spread, 0.0), axis=1, keepdims=True)
    folded[...] = jnp.zeros_like(folded)
    own_sign.wait()
    sign_t[...] = (2 * sign_buf[...] - 1).astype(jnp.float32).T.astype(jnp.bfloat16)

    near = jnp.minimum(me, n - 1 - me)
    longer = 1 - 2 * (me // (n // 2))

    def shard_of(turn):
        far = jnp.minimum(turn // (2 * near + 1), 1)
        return me + jnp.maximum((turn + 1) // 2, turn - near) * ((1 - far) * (2 * (turn % 2) - 1) + far * longer)

    def forward(shard):
        pltpu.make_async_copy(out_all.at[shard], out_all.at[shard], out_recv.at[shard]).wait()

        @pl.when(jnp.logical_and(shard < me, me < n - 1))
        def _():
            out_copy(out_all.at[shard], shard, 0).start()

        @pl.when(jnp.logical_and(shard > me, me > 0))
        def _():
            out_copy(out_all.at[shard], shard, 1).start()

    def fetch(turn):
        paired = jnp.logical_and(turn > 0, turn <= 2 * near)

        @pl.when(jnp.logical_not(jnp.logical_and(paired, turn % 2 == 0)))
        def _():
            forward(shard_of(turn))

        @pl.when(jnp.logical_and(paired, turn % 2 == 1))
        def _():
            forward(shard_of(turn + 1))

        shard = shard_of(turn)
        pltpu.make_async_copy(in_all.at[shard], in_all.at[shard], in_recv.at[shard]).wait()
        position = (iota((docs, tok), 1) + shard * tok).astype(jnp.float32)
        hot = jnp.where(jnp.logical_and(position >= first, position < last), 1.0, 0.0).astype(jnp.bfloat16)
        return shard, jnp.concatenate([hot, hot], axis=1)

    def add_products(shard, hot, group):
        right = out_all[shard]
        left = in_all[shard].astype(jnp.float32)
        col_ids = iota((1, cols), 1)
        signed = [right * pm_one(jnp.bitwise_and(col_ids, group * kper + at)).astype(jnp.bfloat16) for at in range(kper)]
        product = dot(jnp.concatenate(signed, axis=0), sign_t[...])
        for at in range(kper):
            terms = split_terms(product[at * tok:(at + 1) * tok] * left, 2)
            where = pl.ds(pl.multiple_of((group * kper + at) * docs, docs), docs)
            folded[where, :] += dot(hot, jnp.concatenate(terms, axis=0))

    def visit(turn, carry):
        shard, hot = fetch(turn)

        def some(group, carry):
            add_products(shard, hot, group)
            return carry

        return lax.fori_loop(0, kc // kper, some, carry)

    lax.fori_loop(0, n - 1, visit, 0)

    def stage_copy(stage, piece):
        bit = 1 << stage
        partner = me + bit * (1 - 2 * ((me // bit) % 2))
        exact = piece < wide
        return pltpu.make_async_remote_copy(
            src_ref=stage_own.at[stage, piece] if exact else stage_tx.at[stage, piece - wide],
            dst_ref=stage_rx.at[stage, piece] if exact else stage_rx16.at[stage, piece - wide],
            send_sem=st_send.at[stage, piece], recv_sem=st_recv.at[stage, piece],
            device_id={"blk": partner}, device_id_type=MESH)

    def stage_send(stage, piece, value):
        stage_own[stage, piece] = value
        if piece >= wide:
            stage_tx[stage, piece - wide] = value.astype(jnp.bfloat16)
        stage_copy(stage, piece).start()

    def stage_take(stage, piece):
        stage_copy(stage, piece).wait_recv()
        if piece < wide:
            got = stage_rx[stage, piece]
        else:
            got = stage_rx16[stage, piece - wide].astype(jnp.float32)
        keep_sign = (1 - 2 * ((me // (1 << stage)) % 2)).astype(jnp.float32)
        return got + keep_sign * stage_own[stage, piece]

    ksplit = pieces // (rows // 128)
    span = kc // ksplit * docs

    def place(piece):
        return (slice(piece % ksplit * span, (piece % ksplit + 1) * span),
                slice(piece // ksplit * 128, (piece // ksplit + 1) * 128))

    def local_transform(piece):
        total = None
        for term in split_terms(folded[place(piece)[0], :], 3):
            value = dot(term, had[:, place(piece)[1]])
            total = value if total is None else total + value
        stage_send(0, piece, total)

    shard, hot = fetch(n - 1)
    for piece in range(ksplit):
        each = kc // kper // ksplit

        def last_products(group, carry):
            add_products(shard, hot, group)
            return carry

        lax.fori_loop(piece * each, (piece + 1) * each, last_products, 0)
        local_transform(piece)
    for piece in range(ksplit, pieces):
        local_transform(piece)
    for stage in range(stages - 1):
        for piece in range(pieces):
            stage_send(stage + 1, piece, stage_take(stage, piece))

    def feat_copy(which, cut, step):
        to = lax.rem(me + step, n)
        return pltpu.make_async_remote_copy(
            src_ref=feat_tx.at[which, cut, to], dst_ref=feat_rx.at[which, cut, me],
            send_sem=ft_send.at[which, cut, to], recv_sem=ft_recv.at[which, cut, me],
            device_id={"blk": to}, device_id_type=MESH)

    def feat_arrived(which, cut, step):
        source = lax.rem(me + step, n)
        block = feat_rx.at[which, cut, source]
        return pltpu.make_async_copy(block, block, ft_recv.at[which, cut, source])

    def kept_copy(part):
        lines = pl.ds(part * (128 // jl) * docs, 128 // jl * docs)
        return pltpu.make_async_remote_copy(
            src_ref=kept.at[half, lines], dst_ref=kept.at[half, lines],
            send_sem=kept_sem.at[0, part], recv_sem=kept_sem.at[1, part],
            device_id={"sub": other}, device_id_type=MESH)

    kl = 128 // jl
    lane = iota((docs, 128), 1) // jl
    per = depth // gl
    parts = rows // 128
    for row_part in range(parts):
        for piece in range(row_part * ksplit, (row_part + 1) * ksplit):
            folded[place(piece)] = (stage_take(stages - 1, piece) * scale).astype(jnp.bfloat16).astype(jnp.float32)
        base = row_part * 128
        for group in range(row_part * kl, (row_part + 1) * kl):
            tiles = []
            for part in range(gl // 128):
                tile = None
                for at in range(kl):
                    k = part * kl + at
                    piece = folded[k * docs:(k + 1) * docs, base:base + 128]
                    shift = (at * jl - (group * jl - base)) % 128
                    if shift:
                        piece = pltpu.roll(piece, shift, 1)
                    tile = piece if tile is None else jnp.where(lane == at, piece, tile)
                tiles.append(tile)
            line = jnp.concatenate(tiles, axis=1).astype(jnp.bfloat16)
            kept[half, group * docs:(group + 1) * docs, :] = dot(line, perm[...]).astype(jnp.bfloat16)
        kept_copy(row_part).start()

        for turn in range(2):
            which = half if turn == 0 else other
            if turn == 1:
                kept_copy(row_part).wait_recv()
            if row_part == 0:
                own_feat[which] = jnp.zeros((docs, feats), jnp.float32)

            final = row_part == parts - 1
            for cut in range(cuts if final else 1):
                piece_width = feats // cuts if final else feats
                across = slice(cut * piece_width, (cut + 1) * piece_width)

                def slice_step(piece, carry, which=which, cut=cut, across=across):
                    if cut == 0:
                        slab(which, piece).wait()
                    lhs = jnp.concatenate(
                        [kept[which, pl.ds(pl.multiple_of((piece * per + at) * docs, docs), docs), :] for at in range(per)],
                        axis=1)
                    own_feat[which, :, across] += dot(
                        lhs, weights[which, pl.ds(pl.multiple_of(piece * depth, depth), depth), across])
                    return carry

                lax.fori_loop(row_part * (slabs // parts), (row_part + 1) * (slabs // parts), slice_step, 0)
                if final:
                    for owner in range(n):
                        low = own_feat[which, owner * mine:(owner + 1) * mine, cut * piece_width:cut * piece_width + hq]
                        high = own_feat[which, owner * mine:(owner + 1) * mine, cut * piece_width + hq:(cut + 1) * piece_width]
                        feat_tx[which, cut, owner] = jnp.concatenate([low, high], axis=0).astype(jnp.bfloat16)
                    for step in sorted(range(1, n), key=lambda s: -min(s, n - s)):
                        feat_copy(which, cut, step).start()

    at = pl.ds(pl.multiple_of(me * mine, mine), mine)
    for which in range(2):
        for cut in range(cuts):
            for step in range(1, n):
                feat_arrived(which, cut, step).wait()
            begin = cut * 2 * hq
            low = own_feat[which, at, begin:begin + hq]
            high = own_feat[which, at, begin + hq:begin + 2 * hq]
            for step in range(1, n):
                block = feat_rx[which, cut, lax.rem(me + step, n)].astype(jnp.float32)
                low = low + block[:mine]
                high = high + block[mine:]
            feat_ref[:, which, begin:begin + hq] = low
            feat_ref[:, which, begin + hq:begin + 2 * hq] = high

    for shard in range(n):
        @pl.when(jnp.logical_and(shard <= me, me < n - 1))
        def _():
            out_copy(out_all.at[shard], shard, 0).wait_send()

        @pl.when(jnp.logical_and(shard >= me, me > 0))
        def _():
            out_copy(out_all.at[shard], shard, 1).wait_send()

    for step in range(1, n):
        in_copy(step).wait_send()
        for which in range(2):
            for cut in range(cuts):
                feat_copy(which, cut, step).wait_send()
    for stage in range(stages):
        for piece in range(pieces):
            stage_copy(stage, piece).wait_send()
    for part in range(parts):
        kept_copy(part).wait_send()


def sketch(in_factors, out_factors, lengths, signs, projection):
    n = lax.axis_size("blk")
    halves = lax.axis_size("sub")
    layers, _, tok, width = in_factors.shape
    cols = out_factors.shape[3]
    rows = signs.shape[1]
    docs = lengths.shape[1]
    kc = projection.shape[2]
    feats = projection.shape[3]
    scale = 1.0 / math.sqrt(width * cols)
    dims = (n, halves, layers, tok, width, cols, rows, docs, kc, feats, scale)
    stages = n.bit_length() - 1
    parts = rows // 128
    pieces, slabs, gl = 2 * parts, 2 * parts, 256
    wide = pieces // 2
    cuts = 2
    span = kc // 2 * docs
    kdim = rows * kc
    bf16, f32, dma = jnp.bfloat16, jnp.float32, pltpu.SemaphoreType.DMA
    anywhere = pl.BlockSpec(memory_space=pl.ANY)
    vmem = pl.BlockSpec(memory_space=pltpu.VMEM)
    features = pl.pallas_call(
        functools.partial(sketch_kernel, dims),
        out_shape=jax.ShapeDtypeStruct((docs // n, layers, feats), f32),
        in_specs=[vmem, anywhere, anywhere, anywhere, anywhere],
        out_specs=vmem,
        scratch_shapes=[
            pltpu.VMEM((n, tok, rows), bf16),
            pltpu.VMEM((n, tok, cols), bf16),
            pltpu.VMEM((rows, cols), jnp.int32),
            pltpu.VMEM((cols, rows), bf16),
            pltpu.VMEM((rows, rows), bf16),
            pltpu.VMEM((gl, gl), bf16),
            pltpu.VMEM((layers, kdim, feats), bf16),
            pltpu.VMEM((kc * docs, rows), f32),
            pltpu.VMEM((stages, pieces, span, 128), f32),
            pltpu.VMEM((stages, pieces - wide, span, 128), bf16),
            pltpu.VMEM((stages, wide, span, 128), f32),
            pltpu.VMEM((stages, pieces - wide, span, 128), bf16),
            pltpu.VMEM((layers, kdim // gl * docs, gl), bf16),
            pltpu.VMEM((layers, docs, feats), f32),
            pltpu.VMEM((layers, cuts, n, 2 * docs // n, feats // cuts // 2), bf16),
            pltpu.VMEM((layers, cuts, n, 2 * docs // n, feats // cuts // 2), bf16),
            dma((layers, slabs)), dma, dma((n,)), dma((2, n)), dma((n,)), dma((n,)),
            dma((stages, pieces)), dma((stages, pieces)), dma((2, parts)), dma((layers, cuts, n)), dma((layers, cuts, n)),
        ],
        compiler_params=pltpu.CompilerParams(collective_id=0, has_side_effects=True, vmem_limit_bytes=56 << 20),
    )(lengths, in_factors, out_factors, signs, projection.reshape(layers, kdim, feats))
    return features[None]


def pick(in_factors, out_factors, lengths, signs, projection):
    n = lax.axis_size("blk")
    layers, _, tok, width = in_factors.shape
    fits = (
        n > 1 and n & (n - 1) == 0
        and layers == 2 and lax.axis_size("sub") == 2
        and signs.shape[1] % 256 == 0 and tok % 128 == 0
        and lengths.shape[1] % (8 * n) == 0 and projection.shape[2] == 16
        and projection.shape[3] % 512 == 0
        and projection.size * projection.dtype.itemsize <= 36 << 20
    )
    run = sketch if fits else shards
    return run(in_factors, out_factors, lengths, signs, projection)


def solution(mesh):
    return jax.shard_map(
        pick,
        mesh=mesh,
        in_specs=(
            P(None, ("parts", "dp"), "blk", None),
            P(None, ("parts", "dp"), "blk", None),
            P(("parts", "dp"), None),
            P(None, "blk", None),
            P(None, "blk", None, "sub"),
        ),
        out_specs=P(("parts", "dp"), "blk", None, "sub"),
        check_vma=False,
    )
```

```python
import functools
import math

import jax
import jax.numpy as jnp
from jax import lax
from jax.experimental import pallas as pl
from jax.experimental.pallas import tpu as pltpu
from jax.sharding import PartitionSpec as P

MESH = pl.DeviceIdType.MESH


def swapped(block, axis, bit):
    count = lax.axis_size(axis)
    route = []
    for low in range(count):
        high = low | 1 << bit
        if high != low and high < count:
            route += [(low, high), (high, low)]
    return lax.ppermute(block, axis, route)


def parity_sign(values):
    total = jnp.zeros_like(values)
    for bit_level in range(16):
        total = total + jnp.bitwise_and(jnp.right_shift(values, bit_level), 1)
    return (1 - 2 * (total % 2)).astype(jnp.float32)


def parity_table(row_ids, col_ids):
    return parity_sign(jnp.bitwise_and(row_ids[:, None], col_ids[None, :]))


def build_weighted(owners, example_ids, input_cols):
    one_hot = (owners[:, None] == example_ids[None, :]).astype(jnp.bfloat16)
    product = one_hot[None, :, :, None] * input_cols[:, 0, :, None, :]
    return product.reshape(product.shape[0], product.shape[1], product.shape[2] * product.shape[3])


def make_accumulate(weighted, portion):
    return jnp.einsum("ltx,ltc->lxc", weighted, portion[:, 0], preferred_element_type=jnp.float32)


def shards(in_factors, out_factors, lengths, signs, projection):
    blocks = lax.axis_size("blk")
    halves = lax.axis_size("sub")
    my_block = lax.axis_index("blk")
    my_half = lax.axis_index("sub")
    layers = in_factors.shape[0]
    tok_local = in_factors.shape[2]
    in_width = in_factors.shape[3]
    out_width = out_factors.shape[3]
    rows_block = in_width // blocks
    documents = lengths.shape[1]
    kept_cols = projection.shape[2]
    tok_shard = tok_local * blocks
    norm_scale = 1.0 / math.sqrt(in_width * out_width)
    input_cols = lax.all_to_all(in_factors, "blk", split_axis=3, concat_axis=2, tiled=True)
    doc_ends = jnp.cumsum(lengths[0])
    positions = jnp.arange(tok_shard, dtype=jnp.int32)
    owners = jnp.sum((positions[:, None] >= doc_ends[None, :]).astype(jnp.int32), axis=1)
    width_part = out_width // halves
    col_base = my_half * width_part
    example_ids = jnp.arange(documents, dtype=jnp.int32)
    right_part = lax.dynamic_slice_in_dim(out_factors, col_base, width_part, 3)
    weighted = build_weighted(owners, example_ids, input_cols)
    gradients = make_accumulate(weighted, lax.all_gather(right_part, "blk", axis=2, tiled=True))
    gradients = gradients.reshape(layers, documents, rows_block, width_part)
    col_ids = col_base + jnp.arange(width_part, dtype=jnp.int32)
    sign_slice = lax.dynamic_slice_in_dim(signs, col_base, width_part, 2)
    signed = (2 * sign_slice - 1).astype(jnp.float32)
    col_mix = parity_table(col_ids, jnp.arange(kept_cols, dtype=jnp.int32))
    mixing = signed[:, :, :, None] * col_mix[None, None, :, :]
    folded = jnp.einsum("leic,lick->leik", gradients, mixing, precision=lax.Precision.HIGHEST)
    local_rows = jnp.arange(rows_block, dtype=jnp.int32)
    row_mix = parity_table(local_rows, local_rows)
    within = jnp.einsum("ji,leik->lejk", row_mix, folded, precision=lax.Precision.HIGHEST)
    within = within.reshape(layers, documents, rows_block * kept_cols)
    within = lax.psum_scatter(within, "sub", scatter_dimension=1, tiled=True)
    blended = within
    for bit_level in range(blocks.bit_length() - 1):
        partner = swapped(blended, "blk", bit_level)
        high_bit = jnp.bitwise_and(jnp.right_shift(my_block, bit_level), 1)
        blended = partner + (1 - 2 * high_bit).astype(jnp.float32) * blended
    kept_half = (blended * norm_scale).astype(jnp.bfloat16)
    gathered = lax.all_gather(kept_half, "sub", axis=1, tiled=True)
    weights = projection.reshape(layers, rows_block * kept_cols, projection.shape[3])
    features = lax.psum_scatter(
        jnp.einsum("lek,lkp->elp", gathered, weights, preferred_element_type=jnp.float32),
        "blk",
        scatter_dimension=0,
        tiled=True,
    )
    return features[None]


def parity(values):
    for shift in (8, 4, 2, 1):
        values = jnp.bitwise_xor(values, jnp.right_shift(values, shift))
    return jnp.bitwise_and(values, 1)


def pm_one(values):
    return (1 - 2 * parity(values)).astype(jnp.float32)


def iota(shape, axis):
    return lax.broadcasted_iota(jnp.int32, shape, axis)


def split_terms(value, terms):
    parts = []
    for _ in range(terms):
        part = value.astype(jnp.bfloat16)
        parts.append(part)
        value = value - part.astype(jnp.float32)
    return parts


def dot(a, b):
    return jnp.dot(a, b, preferred_element_type=jnp.float32)


def sketch_kernel(dims, len_ref, in_ref, out_ref, signs_ref, proj_ref, feat_ref,
                  in_all, out_all, sign_buf, sign_t, had, perm, weights, folded, stage_own, stage_tx, stage_rx, stage_rx16,
                  kept, own_feat, feat_tx, feat_rx,
                  proj_sem, sign_sem, out_recv, out_send, in_recv, in_send,
                  st_send, st_recv, kept_sem, ft_send, ft_recv):
    n, halves, layers, tok, width, cols, rows, docs, kc, feats, scale = dims
    me = lax.axis_index("blk")
    half = lax.axis_index("sub")
    other = 1 - half
    layer = half
    stages = n.bit_length() - 1
    pieces = stage_own.shape[1]
    kper = 4
    narrow = stage_rx16.shape[1]
    mine = docs // n
    gl = perm.shape[0]
    jl = gl // kc
    groups = rows // jl
    kdim = rows * kc
    cuts = feat_tx.shape[1]
    hq = feats // cuts // 2

    slabs = proj_sem.shape[1]
    depth = kdim // slabs

    def slab(which, piece):
        at = pl.ds(piece * depth, depth)
        return pltpu.make_async_copy(proj_ref.at[which, at], weights.at[which, at], proj_sem.at[which, piece])

    own_out = pltpu.make_async_copy(out_ref.at[layer, 0], out_all.at[me], out_recv.at[me])
    own_in = pltpu.make_async_copy(in_ref.at[layer, 0, :, pl.ds(pl.multiple_of(me * rows, 128), rows)], in_all.at[me], in_recv.at[me])
    own_sign = pltpu.make_async_copy(signs_ref.at[layer], sign_buf, sign_sem)
    own_sign.start()
    own_out.start()
    own_in.start()

    barrier = pltpu.get_barrier_semaphore()
    for step in range(1, n):
        pl.semaphore_signal(barrier, inc=1, device_id={"blk": lax.rem(me + step, n)}, device_id_type=MESH)
    pl.semaphore_signal(barrier, inc=1, device_id={"sub": other}, device_id_type=MESH)
    pl.semaphore_wait(barrier, n)

    def out_copy(src, shard, direction):
        return pltpu.make_async_remote_copy(
            src_ref=src, dst_ref=out_all.at[shard], send_sem=out_send.at[direction, shard], recv_sem=out_recv.at[shard],
            device_id={"blk": me + 1 - 2 * direction}, device_id_type=MESH)

    def in_copy(step):
        to = lax.rem(me + step, n)
        return pltpu.make_async_remote_copy(
            src_ref=in_ref.at[layer, 0, :, pl.ds(pl.multiple_of(to * rows, 128), rows)], dst_ref=in_all.at[me],
            send_sem=in_send.at[to], recv_sem=in_recv.at[me], device_id={"blk": to}, device_id_type=MESH)

    @pl.when(me < n - 1)
    def _():
        out_copy(out_ref.at[layer, 0], me, 0).start()

    @pl.when(me > 0)
    def _():
        out_copy(out_ref.at[layer, 0], me, 1).start()

    for step in sorted(range(1, n), key=lambda s: min(s, n - s)):
        in_copy(step).start()

    had[...] = pm_one(jnp.bitwise_and(iota((rows, rows), 0), iota((rows, rows), 1))).astype(jnp.bfloat16)
    source, target = iota((gl, gl), 0), iota((gl, gl), 1)
    perm[...] = jnp.where((source % jl) * kc + source // jl == target, 1.0, 0.0).astype(jnp.bfloat16)
    spread = jnp.broadcast_to(len_ref[...], (docs, docs)).astype(jnp.float32)
    row_id, col_id = iota((docs, docs), 0), iota((docs, docs), 1)
    first = jnp.sum(jnp.where(col_id < row_id, spread, 0.0), axis=1, keepdims=True)
    last = jnp.sum(jnp.where(col_id <= row_id, spread, 0.0), axis=1, keepdims=True)
    folded[...] = jnp.zeros_like(folded)
    own_sign.wait()
    sign_t[...] = (2 * sign_buf[...] - 1).astype(jnp.float32).T.astype(jnp.bfloat16)

    near = jnp.minimum(me, n - 1 - me)
    longer = 1 - 2 * (me // (n // 2))

    def shard_of(turn):
        far = jnp.minimum(turn // (2 * near + 1), 1)
        return me + jnp.maximum((turn + 1) // 2, turn - near) * ((1 - far) * (2 * (turn % 2) - 1) + far * longer)

    def forward(shard):
        pltpu.make_async_copy(out_all.at[shard], out_all.at[shard], out_recv.at[shard]).wait()

        @pl.when(jnp.logical_and(shard < me, me < n - 1))
        def _():
            out_copy(out_all.at[shard], shard, 0).start()

        @pl.when(jnp.logical_and(shard > me, me > 0))
        def _():
            out_copy(out_all.at[shard], shard, 1).start()

    def fetch(turn):
        paired = jnp.logical_and(turn > 0, turn <= 2 * near)

        @pl.when(jnp.logical_not(jnp.logical_and(paired, turn % 2 == 0)))
        def _():
            forward(shard_of(turn))

        @pl.when(jnp.logical_and(paired, turn % 2 == 1))
        def _():
            forward(shard_of(turn + 1))

        shard = shard_of(turn)
        pltpu.make_async_copy(in_all.at[shard], in_all.at[shard], in_recv.at[shard]).wait()
        position = (iota((docs, tok), 1) + shard * tok).astype(jnp.float32)
        hot = jnp.where(jnp.logical_and(position >= first, position < last), 1.0, 0.0).astype(jnp.bfloat16)
        return shard, jnp.concatenate([hot, hot], axis=1)

    def add_products(shard, hot, group):
        right = out_all[shard]
        left = in_all[shard].astype(jnp.float32)
        col_ids = iota((1, cols), 1)
        signed = [right * pm_one(jnp.bitwise_and(col_ids, group * kper + at)).astype(jnp.bfloat16) for at in range(kper)]
        product = dot(jnp.concatenate(signed, axis=0), sign_t[...])
        for at in range(kper):
            terms = split_terms(product[at * tok:(at + 1) * tok] * left, 2)
            where = pl.ds(pl.multiple_of((group * kper + at) * docs, docs), docs)
            folded[where, :] += dot(hot, jnp.concatenate(terms, axis=0))

    def visit(turn, carry):
        shard, hot = fetch(turn)

        @pl.when(turn == min(1, n - 2))
        def _():
            for piece in range(slabs):
                for which in range(layers):
                    slab(which, piece).start()

        def some(group, carry):
            add_products(shard, hot, group)
            return carry

        return lax.fori_loop(0, kc // kper, some, carry)

    lax.fori_loop(0, n - 1, visit, 0)

    def stage_copy(stage, piece):
        bit = 1 << stage
        partner = me + bit * (1 - 2 * ((me // bit) % 2))
        exact = piece >= narrow
        return pltpu.make_async_remote_copy(
            src_ref=stage_own.at[stage, piece] if exact else stage_tx.at[stage, piece],
            dst_ref=stage_rx.at[stage, piece - narrow] if exact else stage_rx16.at[stage, piece],
            send_sem=st_send.at[stage, piece], recv_sem=st_recv.at[stage, piece],
            device_id={"blk": partner}, device_id_type=MESH)

    def stage_send(stage, piece, value):
        stage_own[stage, piece] = value
        if piece < narrow:
            stage_tx[stage, piece] = value.astype(jnp.bfloat16)
        stage_copy(stage, piece).start()

    def stage_take(stage, piece):
        stage_copy(stage, piece).wait_recv()
        if piece >= narrow:
            got = stage_rx[stage, piece - narrow]
        else:
            got = stage_rx16[stage, piece].astype(jnp.float32)
        keep_sign = (1 - 2 * ((me // (1 << stage)) % 2)).astype(jnp.float32)
        return got + keep_sign * stage_own[stage, piece]

    ksplit = pieces // (rows // 128)
    span = kc // ksplit * docs

    def place(piece):
        return (slice(piece % ksplit * span, (piece % ksplit + 1) * span),
                slice(piece // ksplit * 128, (piece // ksplit + 1) * 128))

    def local_transform(piece):
        total = None
        for term in split_terms(folded[place(piece)[0], :], 3):
            value = dot(term, had[:, place(piece)[1]])
            total = value if total is None else total + value
        stage_send(0, piece, total)

    shard, hot = fetch(n - 1)
    for piece in range(ksplit):
        each = kc // kper // ksplit

        def last_products(group, carry):
            add_products(shard, hot, group)
            return carry

        lax.fori_loop(piece * each, (piece + 1) * each, last_products, 0)
        local_transform(piece)
    for piece in range(ksplit, pieces):
        local_transform(piece)
    for stage in range(stages - 1):
        for piece in range(pieces):
            stage_send(stage + 1, piece, stage_take(stage, piece))

    def feat_copy(which, cut, step):
        to = lax.rem(me + step, n)
        return pltpu.make_async_remote_copy(
            src_ref=feat_tx.at[which, cut, to], dst_ref=feat_rx.at[which, cut, me],
            send_sem=ft_send.at[which, cut, to], recv_sem=ft_recv.at[which, cut, me],
            device_id={"blk": to}, device_id_type=MESH)

    def feat_arrived(which, cut, step):
        source = lax.rem(me + step, n)
        block = feat_rx.at[which, cut, source]
        return pltpu.make_async_copy(block, block, ft_recv.at[which, cut, source])

    def kept_copy(part):
        lines = pl.ds(part * (128 // jl) * docs, 128 // jl * docs)
        return pltpu.make_async_remote_copy(
            src_ref=kept.at[half, lines], dst_ref=kept.at[half, lines],
            send_sem=kept_sem.at[0, part], recv_sem=kept_sem.at[1, part],
            device_id={"sub": other}, device_id_type=MESH)

    kl = 128 // jl
    lane = iota((docs, 128), 1) // jl
    per = depth // gl
    parts = rows // 128
    for row_part in range(parts):
        for piece in range(row_part * ksplit, (row_part + 1) * ksplit):
            folded[place(piece)] = (stage_take(stages - 1, piece) * scale).astype(jnp.bfloat16).astype(jnp.float32)
        base = row_part * 128
        for group in range(row_part * kl, (row_part + 1) * kl):
            tiles = []
            for part in range(gl // 128):
                tile = None
                for at in range(kl):
                    k = part * kl + at
                    piece = folded[k * docs:(k + 1) * docs, base:base + 128]
                    shift = (at * jl - (group * jl - base)) % 128
                    if shift:
                        piece = pltpu.roll(piece, shift, 1)
                    tile = piece if tile is None else jnp.where(lane == at, piece, tile)
                tiles.append(tile)
            line = jnp.concatenate(tiles, axis=1).astype(jnp.bfloat16)
            kept[half, group * docs:(group + 1) * docs, :] = dot(line, perm[...]).astype(jnp.bfloat16)
        kept_copy(row_part).start()

        for turn in range(2):
            which = half if turn == 0 else other
            if turn == 1:
                kept_copy(row_part).wait_recv()
            if row_part == 0:
                own_feat[which] = jnp.zeros((docs, feats), jnp.float32)

            final = row_part == parts - 1
            for cut in range(cuts if final else 1):
                piece_width = feats // cuts if final else feats
                across = slice(cut * piece_width, (cut + 1) * piece_width)

                def slice_step(piece, carry, which=which, cut=cut, across=across):
                    if cut == 0:
                        slab(which, piece).wait()
                    lhs = jnp.concatenate(
                        [kept[which, pl.ds(pl.multiple_of((piece * per + at) * docs, docs), docs), :] for at in range(per)],
                        axis=1)
                    own_feat[which, :, across] += dot(
                        lhs, weights[which, pl.ds(pl.multiple_of(piece * depth, depth), depth), across])
                    return carry

                lax.fori_loop(row_part * (slabs // parts), (row_part + 1) * (slabs // parts), slice_step, 0)
                if final:
                    for owner in range(n):
                        low = own_feat[which, owner * mine:(owner + 1) * mine, cut * piece_width:cut * piece_width + hq]
                        high = own_feat[which, owner * mine:(owner + 1) * mine, cut * piece_width + hq:(cut + 1) * piece_width]
                        feat_tx[which, cut, owner] = jnp.concatenate([low, high], axis=0).astype(jnp.bfloat16)
                    for step in sorted(range(1, n), key=lambda s: -min(s, n - s)):
                        feat_copy(which, cut, step).start()

    at = pl.ds(pl.multiple_of(me * mine, mine), mine)
    for which in range(2):
        for cut in range(cuts):
            for step in range(1, n):
                feat_arrived(which, cut, step).wait()
            begin = cut * 2 * hq
            low = own_feat[which, at, begin:begin + hq]
            high = own_feat[which, at, begin + hq:begin + 2 * hq]
            for step in range(1, n):
                block = feat_rx[which, cut, lax.rem(me + step, n)].astype(jnp.float32)
                low = low + block[:mine]
                high = high + block[mine:]
            feat_ref[:, which, begin:begin + hq] = low
            feat_ref[:, which, begin + hq:begin + 2 * hq] = high

    for shard in range(n):
        @pl.when(jnp.logical_and(shard <= me, me < n - 1))
        def _():
            out_copy(out_all.at[shard], shard, 0).wait_send()

        @pl.when(jnp.logical_and(shard >= me, me > 0))
        def _():
            out_copy(out_all.at[shard], shard, 1).wait_send()

    for step in range(1, n):
        in_copy(step).wait_send()
        for which in range(2):
            for cut in range(cuts):
                feat_copy(which, cut, step).wait_send()
    for stage in range(stages):
        for piece in range(pieces):
            stage_copy(stage, piece).wait_send()
    for part in range(parts):
        kept_copy(part).wait_send()


def sketch(in_factors, out_factors, lengths, signs, projection):
    n = lax.axis_size("blk")
    halves = lax.axis_size("sub")
    layers, _, tok, width = in_factors.shape
    cols = out_factors.shape[3]
    rows = signs.shape[1]
    docs = lengths.shape[1]
    kc = projection.shape[2]
    feats = projection.shape[3]
    scale = 1.0 / math.sqrt(width * cols)
    dims = (n, halves, layers, tok, width, cols, rows, docs, kc, feats, scale)
    stages = n.bit_length() - 1
    parts = rows // 128
    pieces, slabs, gl = 2 * parts, 2 * parts, 256
    wide = pieces // 2
    cuts = 2
    span = kc // 2 * docs
    kdim = rows * kc
    bf16, f32, dma = jnp.bfloat16, jnp.float32, pltpu.SemaphoreType.DMA
    anywhere = pl.BlockSpec(memory_space=pl.ANY)
    vmem = pl.BlockSpec(memory_space=pltpu.VMEM)
    features = pl.pallas_call(
        functools.partial(sketch_kernel, dims),
        out_shape=jax.ShapeDtypeStruct((docs // n, layers, feats), f32),
        in_specs=[vmem, anywhere, anywhere, anywhere, anywhere],
        out_specs=vmem,
        scratch_shapes=[
            pltpu.VMEM((n, tok, rows), bf16),
            pltpu.VMEM((n, tok, cols), bf16),
            pltpu.VMEM((rows, cols), jnp.int32),
            pltpu.VMEM((cols, rows), bf16),
            pltpu.VMEM((rows, rows), bf16),
            pltpu.VMEM((gl, gl), bf16),
            pltpu.VMEM((layers, kdim, feats), bf16),
            pltpu.VMEM((kc * docs, rows), f32),
            pltpu.VMEM((stages, pieces, span, 128), f32),
            pltpu.VMEM((stages, pieces - wide, span, 128), bf16),
            pltpu.VMEM((stages, wide, span, 128), f32),
            pltpu.VMEM((stages, pieces - wide, span, 128), bf16),
            pltpu.VMEM((layers, kdim // gl * docs, gl), bf16),
            pltpu.VMEM((layers, docs, feats), f32),
            pltpu.VMEM((layers, cuts, n, 2 * docs // n, feats // cuts // 2), bf16),
            pltpu.VMEM((layers, cuts, n, 2 * docs // n, feats // cuts // 2), bf16),
            dma((layers, slabs)), dma, dma((n,)), dma((2, n)), dma((n,)), dma((n,)),
            dma((stages, pieces)), dma((stages, pieces)), dma((2, parts)), dma((layers, cuts, n)), dma((layers, cuts, n)),
        ],
        compiler_params=pltpu.CompilerParams(collective_id=0, has_side_effects=True, vmem_limit_bytes=56 << 20),
    )(lengths, in_factors, out_factors, signs, projection.reshape(layers, kdim, feats))
    return features[None]


def pick(in_factors, out_factors, lengths, signs, projection):
    n = lax.axis_size("blk")
    layers, _, tok, width = in_factors.shape
    fits = (
        n > 1 and n & (n - 1) == 0
        and layers == 2 and lax.axis_size("sub") == 2
        and signs.shape[1] % 256 == 0 and tok % 128 == 0
        and lengths.shape[1] % (8 * n) == 0 and projection.shape[2] == 16
        and projection.shape[3] % 512 == 0
        and projection.size * projection.dtype.itemsize <= 36 << 20
    )
    run = sketch if fits else shards
    return run(in_factors, out_factors, lengths, signs, projection)


def solution(mesh):
    return jax.shard_map(
        pick,
        mesh=mesh,
        in_specs=(
            P(None, ("parts", "dp"), "blk", None),
            P(None, ("parts", "dp"), "blk", None),
            P(("parts", "dp"), None),
            P(None, "blk", None),
            P(None, "blk", None, "sub"),
        ),
        out_specs=P(("parts", "dp"), "blk", None, "sub"),
        check_vma=False,
    )
```
